32 devices in a mesh: dp: 4 (over z), ctx: 8 (over y, x, core).
Axes of the slice: x: 2, y: 2, z: 4, core: 2. Of those that a mesh axis runs over, the one named last changes fastest.
Arguments:
- streams: bfloat16 [3, 1, 2560, 8192], P(None, None, 'ctx', 'dp'), may hold values from -6 to 6
- cotangent: bfloat16 [1, 2560, 8192], P(None, 'ctx', 'dp'), may hold values from -6 to 6
- counts: int32 [1, 8], P(None, 'ctx'), may hold values from 1 to 320, as said below
- short_filters: bfloat16 [3, 7, 8192], P(None, None, ('dp', 'ctx')), may hold values from -14 to 14
- long_filter: bfloat16 [128, 8192], P(None, ('dp', 'ctx')), may hold values from -0.5 to 0.5
Outputs:
- stream_grads: bfloat16 [3, 1, 2560, 8192], P(None, None, 'ctx', 'dp')
- long_grad: float32 [128, 8192], P(None, ('dp', 'ctx'))
- short_grad: float32 [3, 7, 8192], P(None, None, ('dp', 'ctx'))
The draws below stay inside these ranges and needn't reach their ends.
Inputs may be any that keep to these rules, and one draw needn't show every extreme that they name: In each window the counts sum to 2048, and one of them equals 320.
All inputs are finite; a program needn't handle non-finite values.
Results may differ from the reference program's by a relative error of at most 0.0058.
Values may be sent and summed in bfloat16 or wider, within the bound.
A program may use at most 128 MiB of HBM per device.

```python
import math
import jax
import jax.numpy as jnp
from jax import lax

CH = 8192
LTAP = 128
STAP = 7
SEQS = 1
CAP = 320
SEQ_LEN = 2048
ROWS = 2560
N_CTX = 8


def draw_short_filters(key, part):
    ramp = jnp.exp(math.log(3.0) * jnp.arange(CH, dtype=jnp.float32) / float(CH))
    base = jnp.clip(jax.random.normal(key, (3, STAP, CH), jnp.float32), -4.0, 4.0)
    return (base * ramp[None, None, :] / math.sqrt(STAP)).astype(jnp.bfloat16)


def drifting_level(key, shape_lead):
    keys = jax.random.split(jax.random.fold_in(key, 71), 3)
    level = jax.random.uniform(keys[0], shape_lead + (1, CH), jnp.float32, 0.3, 0.6)
    waves = jax.random.randint(keys[1], shape_lead + (1, CH), 1, 4).astype(jnp.float32)
    phase = jax.random.uniform(keys[2], shape_lead + (1, CH), jnp.float32, -math.pi, math.pi)
    position = jnp.arange(ROWS, dtype=jnp.float32) / float(ROWS)
    position = position.reshape((1,) * len(shape_lead) + (ROWS, 1))
    return level * (1.0 + 0.5 * jnp.sin(2.0 * math.pi * waves * position + phase))


def rough_part(key, shape):
    noise_key = jax.random.fold_in(key, 73)
    return jnp.clip(jax.random.normal(noise_key, shape, jnp.float32), -4.0, 4.0)


def draw_streams(key, part):
    shape = (3, SEQS, ROWS, CH)
    values = rough_part(key, shape) + drifting_level(key, (3, SEQS))
    return values.astype(jnp.bfloat16)


def draw_cotangent(key, part):
    shape = (SEQS, ROWS, CH)
    values = rough_part(key, shape) + drifting_level(key, (SEQS,))
    return values.astype(jnp.bfloat16)


def count_row(key, run):
    keys = jax.random.split(key, 6)
    others = N_CTX - run
    spread = others - 1
    half = spread // 2
    start = jax.random.randint(keys[0], (), 1, N_CTX - run).astype(jnp.int32)
    tiny = jax.random.randint(keys[1], (run,), 1, 3).astype(jnp.int32)
    tiny = tiny.at[0].set(1)
    rest = SEQ_LEN - CAP - jnp.sum(tiny)
    base = rest // spread
    extra = rest - base * spread
    order_a = jax.random.permutation(keys[2], spread).astype(jnp.int32)
    values = base + (order_a < extra).astype(jnp.int32)
    limit = jnp.maximum(jnp.minimum(CAP - base - 1, base - 1), 0)
    moves = jax.random.randint(keys[3], (half,), 0, limit + 1).astype(jnp.int32)
    delta = jnp.concatenate([moves, jnp.zeros((spread - 2 * half,), jnp.int32), -moves[::-1]])
    order_b = jax.random.permutation(keys[4], spread).astype(jnp.int32)
    values = values + delta[order_b]
    full_at = jax.random.randint(keys[5], (), 0, others).astype(jnp.int32)
    slot = jnp.arange(others, dtype=jnp.int32)
    pick = jnp.clip(slot - (slot > full_at).astype(jnp.int32), 0, spread - 1)
    other_values = jnp.where(slot == full_at, CAP, values[pick])
    device_ids = jnp.arange(N_CTX, dtype=jnp.int32)
    in_run = (device_ids >= start) & (device_ids < start + run)
    run_index = jnp.clip(device_ids - start, 0, run - 1)
    other_index = jnp.clip(jnp.where(device_ids < start, device_ids, device_ids - run), 0, others - 1)
    return jnp.where(in_run, tiny[run_index], other_values[other_index]).astype(jnp.int32)


def draw_counts(key, part):
    run = max(1, N_CTX // 8)
    windows = []
    for window_index in range(SEQS):
        windows.append(count_row(jax.random.fold_in(key, 11 + window_index), run))
    return jnp.stack(windows).astype(jnp.int32)


def block_scale(rng, dims, shards, smallest, largest):
    def one(dim, blocks):
        heights = jax.random.uniform(jax.random.fold_in(jax.random.fold_in(rng, 6), dim), (blocks,), jnp.float32, smallest / len(shards), largest / len(shards))
        return jnp.repeat(jnp.exp(heights), dims[dim] // blocks).reshape((-1,) + (1,) * (len(dims) - dim - 1))

    level = one(*shards[0])
    for cut in shards[1:]:
        level = level * one(*cut)
    return level


def centred(stream_key, shape, width, bound, pieces=(), kind=jnp.bfloat16):
    entries = width * jax.random.normal(stream_key, shape, jnp.float32)
    if pieces:
        entries = entries * block_scale(stream_key, shape, pieces, -0.22, 0.18)
    return jnp.clip(entries, -bound, bound).astype(kind)


def setup_inputs(seed: int = 0) -> dict:
    key_list = jax.random.split(jax.random.key(seed), 6)
    streams = draw_streams(jax.random.fold_in(key_list[5], 71), 0)
    cotangent = draw_cotangent(jax.random.fold_in(key_list[5], 71), 0)
    counts = draw_counts(jax.random.fold_in(key_list[5], 71), 0)
    short_filters = draw_short_filters(jax.random.fold_in(key_list[5], 71), 0)
    long_filter = centred(key_list[4], (LTAP, CH), LTAP ** -0.5, 0.5, ((1, 32),))
    return dict(streams=streams, cotangent=cotangent, counts=counts, short_filters=short_filters, long_filter=long_filter)


def causal_long(lead, filt, length):
    reach = filt.shape[0] - 1

    def add_tap(tap_index, total):
        piece = lax.dynamic_slice_in_dim(lead, reach - tap_index, length, 0)
        return total + filt[tap_index].astype(jnp.float32)[None, :] * piece.astype(jnp.float32)
    return lax.fori_loop(0, filt.shape[0], add_tap, jnp.zeros((length, filt.shape[1]), jnp.float32))

def anticausal_long(trail, filt, length):

    def add_tap(tap_index, total):
        piece = lax.dynamic_slice_in_dim(trail, tap_index, length, 0)
        return total + filt[tap_index].astype(jnp.float32)[None, :] * piece.astype(jnp.float32)
    return lax.fori_loop(0, filt.shape[0], add_tap, jnp.zeros((length, filt.shape[1]), jnp.float32))

def tap_products(lead, grad_rows, taps):
    reach = taps - 1
    length = grad_rows.shape[0]

    def one_tap(tap_index):
        piece = lax.dynamic_slice_in_dim(lead, reach - tap_index, length, 0)
        return lax.optimization_barrier(jnp.sum(grad_rows.astype(jnp.float32) * piece.astype(jnp.float32), axis=0))
    return lax.map(one_tap, jnp.arange(taps, dtype=jnp.int32))

def short_forward(leading, filters, length):
    taps = filters.shape[1]
    summed = jnp.zeros((filters.shape[0], length, filters.shape[2]), jnp.float32)
    for tap_index in range(taps):
        start = taps - 1 - tap_index
        summed = summed + filters[:, tap_index][:, None, :].astype(jnp.float32) * leading[:, start:start + length].astype(jnp.float32)
    return summed

def short_backward(trailing, filters, length):
    taps = filters.shape[1]
    summed = jnp.zeros((filters.shape[0], length, filters.shape[2]), jnp.float32)
    for tap_index in range(taps):
        summed = summed + filters[:, tap_index][:, None, :].astype(jnp.float32) * trailing[:, tap_index:tap_index + length].astype(jnp.float32)
    return summed

def reference(streams, cotangent, counts, short_filters, long_filter):
    reach = LTAP - 1
    short_reach = STAP - 1

    def one_window(items):
        stream, grad_out, live_count = items
        offsets = jnp.cumsum(live_count) - live_count
        slot_ids = jnp.arange(CAP, dtype=jnp.int32)
        where_to = jnp.where(slot_ids[None, :] < live_count[:, None], offsets[:, None] + slot_ids[None, :], SEQ_LEN).reshape(-1).astype(jnp.int32)
        packed = jnp.zeros((3, SEQ_LEN, CH), jnp.bfloat16).at[:, where_to].set(stream, mode='drop')
        packed_dy = jnp.zeros((SEQ_LEN, CH), jnp.bfloat16).at[where_to].set(grad_out, mode='drop')
        leading = jnp.concatenate([jnp.zeros((3, short_reach, CH), jnp.bfloat16), packed], axis=1)
        feats = short_forward(leading, short_filters, SEQ_LEN)
        query, keys, values = (feats[0], feats[1], feats[2])
        gated = (keys * values).astype(jnp.bfloat16)
        gated_lead = jnp.concatenate([jnp.zeros((reach, CH), jnp.bfloat16), gated], axis=0)
        long_out = causal_long(gated_lead, long_filter, SEQ_LEN)
        grad_query = (packed_dy * long_out).astype(jnp.bfloat16)
        grad_long = (packed_dy * query).astype(jnp.bfloat16)
        trailing = jnp.concatenate([grad_long, jnp.zeros((reach, CH), jnp.bfloat16)], axis=0)
        grad_gated = anticausal_long(trailing, long_filter, SEQ_LEN)
        grad_keys = (grad_gated * values).astype(jnp.bfloat16)
        grad_values = (grad_gated * keys).astype(jnp.bfloat16)
        grads = jnp.stack([grad_query, grad_keys, grad_values])
        grad_trail = jnp.concatenate([grads, jnp.zeros((3, short_reach, CH), jnp.bfloat16)], axis=1)
        back = short_backward(grad_trail, short_filters, SEQ_LEN).astype(jnp.bfloat16)
        long_term = tap_products(gated_lead, grad_long, LTAP)
        short_terms = []
        for tap_index in range(STAP):
            start = short_reach - tap_index
            short_terms.append(lax.optimization_barrier(jnp.sum(grads.astype(jnp.float32) * leading[:, start:start + SEQ_LEN].astype(jnp.float32), axis=1)))
        short_term = jnp.stack(short_terms, axis=1)
        back_rows = jnp.concatenate([back, jnp.zeros((3, 1, CH), jnp.bfloat16)], axis=1)
        return (back_rows[:, where_to], long_term, short_term)
    slots_out, long_terms, short_terms = lax.map(one_window, (jnp.transpose(streams, (1, 0, 2, 3)), cotangent, counts))
    stream_grads = jnp.transpose(slots_out, (1, 0, 2, 3))
    long_raw = lax.optimization_barrier(jnp.sum(long_terms, axis=0))
    short_raw = lax.optimization_barrier(jnp.sum(short_terms, axis=0))
    total = jnp.sum(long_raw * long_raw) + jnp.sum(short_raw * short_raw)
    rms = jnp.sqrt(total / float((LTAP + 3 * STAP) * CH) + 1e-06)
    return (stream_grads, long_raw / rms, short_raw / rms)
```

```python
import functools

import jax
import jax.numpy as jnp
import numpy as np
from jax import lax
from jax.experimental import pallas as pl
from jax.experimental.pallas import tpu as pltpu
from jax.sharding import PartitionSpec as P

CH = 8192
LTAP = 128
STAP = 7
MEAN_COUNT = 256
REACH = LTAP - 1 + STAP - 1
N = 480
HALF = N // 2
LEAD = 136
TRAIL = 464
SHORT = 336
ZLEAD = 128
GROWS = 152
F32 = jnp.float32
BF16 = jnp.bfloat16


def ceil16(rows):
    return -(-rows // 16) * 16


def halo_plan(devices, cap):
    slack = devices * cap - devices * MEAN_COUNT
    plan = []
    for distance in range(1, devices):
        nearer = max(distance - 1, (distance - 1) * cap - slack)
        if nearer >= REACH:
            break
        big = ceil16(REACH - nearer)
        small = 16 if nearer < STAP - 1 else 0
        plan.append((big, small))
    return plan


def split(matrix):
    high = matrix.astype(BF16)
    low = (matrix - high.astype(np.float64)).astype(BF16)
    return high, low


def transforms():
    freq = (2.0 * np.pi / N) * (np.arange(HALF) + 0.5)[:, None]

    def forward(first, rows):
        angle = freq * (first + np.arange(rows))[None, :]
        return np.concatenate([np.cos(angle), -np.sin(angle)], axis=0)

    back = forward(0, SHORT).T * (2.0 / N)
    return split(forward(-ZLEAD, TRAIL)) + split(forward(0, TRAIL)) + split(back)


def dot(a, b):
    return jnp.dot(a, b, preferred_element_type=F32)


def chunks(rows, size=32):
    return [(start, min(size, rows - start)) for start in range(0, rows, size)]


def block_kernel(plan, cap, info, *refs):
    tails = refs[: len(plan)]
    heads = refs[len(plan) : 2 * len(plan)]
    refs = refs[2 * len(plan) :]
    (streams, dy_in, filt, fz_hi, fz_lo, fd_hi, fd_lo, g_hi, g_lo) = refs[:9]
    grads_out, sums_out = refs[9:11]
    refs = refs[11:]
    (kw, vw, qw, dyw, ks, vs, zs, dyl, dyl_own, zh, hh, dh, dho, p_hi, p_lo, yz, dm) = refs[:17]
    before = refs[17 : 17 + len(plan)]
    after = refs[17 + len(plan) : 17 + 2 * len(plan)]
    before_q = refs[17 + 2 * len(plan)]
    cols = streams.shape[-1]
    count = info[0]
    remaining = info[1]

    @pl.when(pl.program_id(0) == 0)
    def _():
        for at, (big, small) in enumerate(plan):
            base, live = info[2 + 4 * at], info[3 + 4 * at]
            col = lax.broadcasted_iota(jnp.int32, (LEAD, big), 1)
            row = lax.broadcasted_iota(jnp.int32, (LEAD, big), 0)
            hit = (row - LEAD == col - big - base) & (big - col <= live)
            before[at][...] = jnp.where(hit, 1.0, 0.0).astype(BF16)
            if small:
                col = lax.broadcasted_iota(jnp.int32, (16, 16), 1)
                row = lax.broadcasted_iota(jnp.int32, (16, 16), 0)
                hit = (row == col - base) & (16 - col <= live)
                before_q[at] = jnp.where(hit, 1.0, 0.0).astype(BF16)
            base, live = info[4 + 4 * at], info[5 + 4 * at]
            col = lax.broadcasted_iota(jnp.int32, (TRAIL, big), 1)
            row = lax.broadcasted_iota(jnp.int32, (TRAIL, big), 0)
            hit = (row == col + base) & (col < live)
            after[at][...] = jnp.where(hit, 1.0, 0.0).astype(BF16)

    with jax.named_scope("windows"):
        for which, window in ((0, kw), (1, vw)):
            lead = None
            trail = None
            for at, (big, small) in enumerate(plan):
                part = dot(before[at][...], tails[at][which * big : (which + 1) * big, :])
                lead = part if lead is None else lead + part
                if small:
                    first = 2 * big + which * 16
                    part = dot(after[at][:SHORT, :16], heads[at][first : first + 16, :])
                    trail = part if trail is None else trail + part
            window[:LEAD, :] = lead
            window[LEAD:, :] = trail
            for start, size in chunks(cap):
                row = lax.broadcasted_iota(jnp.int32, (size, 1), 0) + start
                own = streams[1 + which, 0, start : start + size, :].astype(F32)
                window[LEAD + start : LEAD + start + size, :] += jnp.where(row < count, own, 0.0)
        lead = None
        for at, (big, small) in enumerate(plan):
            if small:
                part = dot(before_q[at], tails[at][2 * big : 2 * big + 16, :])
                lead = part if lead is None else lead + part
        qw[:8, :] = lead[8:]
        for which, window, first in ((0, qw, 8), (1, dyw, 0)):
            trail = None
            for at, (big, small) in enumerate(plan):
                part = dot(after[at][...], heads[at][which * big : (which + 1) * big, :])
                trail = part if trail is None else trail + part
            window[first:, :] = trail
            for start, size in chunks(cap):
                row = lax.broadcasted_iota(jnp.int32, (size, 1), 0) + start
                source = streams[0, 0, start : start + size, :] if which == 0 else dy_in[0, start : start + size, :]
                window[first + start : first + start + size, :] += jnp.where(
                    row < count, source.astype(F32), 0.0
                )

    taps = filt[LTAP : LTAP + 32, :].astype(F32)

    def tap(stream, index):
        at = stream * STAP + index
        return taps[at : at + 1, :]

    def causal(window, stream, start, size):
        rows = window[start : start + size + 8, :]
        total = tap(stream, 0) * rows[8:, :]
        for index in range(1, STAP):
            total = total + tap(stream, index) * rows[8 - index : 8 - index + size, :]
        return total

    with jax.named_scope("short_forward"):
        for start, size in chunks(TRAIL):
            span = slice(start, start + size)
            keys = causal(kw, 1, start, size)
            values = causal(vw, 2, start, size)
            ks[span, :] = keys
            vs[span, :] = values
            zs[span, :] = (keys * values).astype(BF16)
        for start, size in chunks(TRAIL):
            span = slice(start, start + size)
            grad = (dyw[span, :] * causal(qw, 0, start, size)).astype(BF16)
            dyl[span, :] = grad
            if start < cap:
                row = lax.broadcasted_iota(jnp.int32, (size, 1), 0) + start
                dyl_own[span, :] = jnp.where(row < count, grad.astype(F32), 0.0).astype(BF16)

    with jax.named_scope("transforms"):
        long = filt[:LTAP, :]
        zh[...] = dot(fz_hi[...], zs[...]) + dot(fz_lo[...], zs[...])
        hh[...] = dot(fd_hi[:, :LTAP], long) + dot(fd_lo[:, :LTAP], long)
        dh[...] = dot(fd_hi[...], dyl[...]) + dot(fd_lo[...], dyl[...])
        dho[...] = dot(fd_hi[:, :cap], dyl_own[...]) + dot(fd_lo[:, :cap], dyl_own[...])

    def product(a, b, conjugate):
        for start, size in chunks(HALF, 16):
            real, imag = slice(start, start + size), slice(HALF + start, HALF + start + size)
            ar, ai, br, bi = a[real, :], a[imag, :], b[real, :], b[imag, :]
            if conjugate:
                cr, ci = ar * br + ai * bi, ai * br - ar * bi
            else:
                cr, ci = ar * br - ai * bi, ai * br + ar * bi
            for span, part in ((real, cr), (imag, ci)):
                high = part.astype(BF16)
                p_hi[span, :] = high
                p_lo[span, :] = (part - high.astype(F32)).astype(BF16)

    def inverse(rows):
        return (
            dot(g_hi[:rows, :], p_hi[...])
            + dot(g_lo[:rows, :], p_hi[...])
            + dot(g_hi[:rows, :], p_lo[...])
        )

    with jax.named_scope("long_filter_grad"):
        product(dho, zh, True)
        sums_out[:LTAP, :] = inverse(LTAP)

    with jax.named_scope("long_forward"):
        product(zh, hh, False)
        yz[...] = inverse(SHORT)
        for start, size in chunks(SHORT):
            span = slice(start, start + size)
            dm[0, span, :] = (dyw[span, :] * yz[span, :]).astype(BF16).astype(F32)

    with jax.named_scope("long_backward"):
        product(dh, hh, True)
        yz[...] = inverse(SHORT)
        for start, size in chunks(SHORT):
            span = slice(start, start + size)
            own = slice(ZLEAD + start, ZLEAD + start + size)
            row = lax.broadcasted_iota(jnp.int32, (size, 1), 0) + start
            grad = jnp.where(row < remaining, yz[span, :], 0.0)
            dm[1, span, :] = (grad * vs[own, :]).astype(BF16).astype(F32)
            dm[2, span, :] = (grad * ks[own, :]).astype(BF16).astype(F32)

    with jax.named_scope("short_backward"):
        for stream, window, lead in ((0, qw, 8), (1, kw, LEAD), (2, vw, LEAD)):
            partial = [jnp.zeros((8, cols), F32) for _ in range(STAP)]
            for start, size in chunks(cap):
                row = lax.broadcasted_iota(jnp.int32, (size, 1), 0) + start
                rows = dm[stream, start : start + size + 8, :]
                total = tap(stream, 0) * rows[:size, :]
                for index in range(1, STAP):
                    total = total + tap(stream, index) * rows[index : index + size, :]
                grads_out[stream, 0, start : start + size, :] = jnp.where(
                    row < count, total, 0.0
                ).astype(BF16)
                mine = jnp.where(row < count, rows[:size, :], 0.0)
                source = window[lead + start - 8 : lead + start + size, :]
                for index in range(STAP):
                    terms = mine * source[8 - index : 8 - index + size, :]
                    for at in range(0, size, 8):
                        partial[index] = partial[index] + terms[at : at + 8, :]
            for index in range(STAP):
                at = LTAP + stream * STAP + index
                sums_out[at : at + 1, :] = jnp.sum(partial[index], axis=0, keepdims=True)
        used = LTAP + 3 * STAP
        sums_out[used:, :] = jnp.zeros((GROWS - used, cols), F32)


def run_blocks(plan, info, tails, heads, streams, cotangent, filters, width=256):
    cap, channels = streams.shape[2:]
    width = min(width, channels)
    matrices = transforms()

    def by_block(rows):
        return pl.BlockSpec((rows, width), lambda step: (0, step))

    whole = [pl.BlockSpec(matrix.shape, lambda step: (0, 0)) for matrix in matrices]
    f32_rows = [
        LEAD + SHORT, LEAD + SHORT, 8 + TRAIL, TRAIL, TRAIL, TRAIL,
    ]
    scratch = [pltpu.VMEM((rows, width), F32) for rows in f32_rows]
    scratch += [pltpu.VMEM((rows, width), BF16) for rows in (TRAIL, TRAIL, cap)]
    scratch += [pltpu.VMEM((N, width), F32) for _ in range(4)]
    scratch += [pltpu.VMEM((N, width), BF16) for _ in range(2)]
    scratch += [pltpu.VMEM((SHORT, width), F32), pltpu.VMEM((3, SHORT, width), F32)]
    scratch += [pltpu.VMEM((LEAD, big), BF16) for big, _ in plan]
    scratch += [pltpu.VMEM((TRAIL, big), BF16) for big, _ in plan]
    scratch += [pltpu.VMEM((len(plan), 16, 16), BF16)]
    return pl.pallas_call(
        functools.partial(block_kernel, plan, cap),
        grid=(channels // width,),
        in_specs=[pl.BlockSpec(memory_space=pltpu.SMEM)]
        + [by_block(part.shape[0]) for part in tails + heads]
        + [
            pl.BlockSpec((3, 1, cap, width), lambda step: (0, 0, 0, step)),
            pl.BlockSpec((1, cap, width), lambda step: (0, 0, step)),
            by_block(filters.shape[0]),
        ]
        + whole,
        out_specs=[
            pl.BlockSpec((3, 1, cap, width), lambda step: (0, 0, 0, step)),
            by_block(GROWS),
        ],
        out_shape=[
            jax.ShapeDtypeStruct(streams.shape, BF16),
            jax.ShapeDtypeStruct((GROWS, channels), F32),
        ],
        scratch_shapes=scratch,
        compiler_params=pltpu.CompilerParams(vmem_limit_bytes=48 * 1024 * 1024),
        name="hyena_blocks",
    )(info, *tails, *heads, streams, cotangent, filters, *[jnp.asarray(m) for m in matrices])


def last_rows(block, live_count, length):
    zero_rows = jnp.zeros(block.shape[:-2] + (length, block.shape[-1]), block.dtype)
    padded = jnp.concatenate([zero_rows, block], axis=-2)
    return lax.dynamic_slice_in_dim(padded, live_count, length, axis=block.ndim - 2)


def halo_info(counts, me, plan):
    devices = counts.shape[0]
    ids = jnp.arange(devices, dtype=jnp.int32)

    def total(first, end):
        return jnp.sum(jnp.where((ids >= first) & (ids < end), counts, 0))

    numbers = [total(me, me + 1), total(me, devices)]
    for distance in range(1, len(plan) + 1):
        numbers += [
            total(me - distance + 1, me),
            total(me - distance, me - distance + 1),
            total(me, me + distance),
            total(me + distance, me + distance + 1),
        ]
    return jnp.stack(numbers).astype(jnp.int32)


def local(streams, cotangent, counts, short_filters, long_filter):
    devices = lax.axis_size("ctx")
    me = lax.axis_index("ctx")
    live_count = counts[0, 0]
    cap = streams.shape[2]
    share = long_filter.shape[1]
    plan = halo_plan(devices, cap)
    q0, k0, v0 = streams[0, 0], streams[1, 0], streams[2, 0]
    dy = cotangent[0]
    digits = jnp.stack([live_count // 16, live_count % 16]).astype(BF16)
    packed = jnp.concatenate(
        [
            long_filter,
            short_filters.reshape(3 * STAP, share),
            jnp.broadcast_to(digits[:, None], (2, share)),
            jnp.zeros((160 - LTAP - 3 * STAP - 2, share), BF16),
        ],
        axis=0,
    )
    filters = lax.all_gather(packed, "ctx", axis=1, tiled=True)
    digits = filters[LTAP + 3 * STAP : LTAP + 3 * STAP + 2, ::share].astype(jnp.int32)
    info = halo_info(digits[0] * 16 + digits[1], me, plan)
    widest = plan[0][0]
    tail = last_rows(streams[:, 0], live_count, widest)
    tails, heads = [], []
    for at, (big, small) in enumerate(plan):
        distance = at + 1
        later = [(j, j + distance) for j in range(devices - distance)]
        earlier = [(j + distance, j) for j in range(devices - distance)]
        last = [tail[1, widest - big :], tail[2, widest - big :]]
        first = [q0[:big], dy[:big]]
        if small:
            last.append(tail[0, widest - small :])
            first += [k0[:small], v0[:small]]
        tails.append(lax.ppermute(jnp.concatenate(last, axis=0), "ctx", later))
        heads.append(lax.ppermute(jnp.concatenate(first, axis=0), "ctx", earlier))
    stream_grads, sums = run_blocks(plan, info, tails, heads, streams, cotangent, filters)
    own = lax.psum_scatter(sums, "ctx", scatter_dimension=1, tiled=True)
    squares = lax.psum(jnp.sum(own * own), ("dp", "ctx"))
    rms = jnp.sqrt(squares / float((LTAP + 3 * STAP) * CH) + 1e-06)
    normed = own / rms
    long_grad = normed[:LTAP]
    short_grad = normed[LTAP : LTAP + 3 * STAP].reshape(3, STAP, share)
    return (stream_grads, long_grad, short_grad)


def solution(mesh):
    return jax.shard_map(
        local,
        mesh=mesh,
        in_specs=(
            P(None, None, "ctx", "dp"),
            P(None, "ctx", "dp"),
            P(None, "ctx"),
            P(None, None, ("dp", "ctx")),
            P(None, ("dp", "ctx")),
        ),
        out_specs=(
            P(None, None, "ctx", "dp"),
            P(None, ("dp", "ctx")),
            P(None, None, ("dp", "ctx")),
        ),
        check_vma=False,
    )
```

```python
import functools

import jax
import jax.numpy as jnp
import numpy as np
from jax import lax
from jax.experimental import pallas as pl
from jax.experimental.pallas import tpu as pltpu
from jax.sharding import PartitionSpec as P

CH = 8192
LTAP = 128
STAP = 7
MEAN_COUNT = 256
REACH = LTAP - 1 + STAP - 1
N = 480
HALF = N // 2
LEAD = 136
TRAIL = 464
SHORT = 336
ZLEAD = 128
GROWS = 160
F32 = jnp.float32
BF16 = jnp.bfloat16


def ceil16(rows):
    return -(-rows // 16) * 16


def halo_plan(devices, cap):
    slack = devices * cap - devices * MEAN_COUNT
    plan = []
    for distance in range(1, devices):
        nearer = max(distance - 1, (distance - 1) * cap - slack)
        if nearer >= REACH:
            break
        big = ceil16(REACH - nearer)
        small = 16 if nearer < STAP - 1 else 0
        plan.append((big, small))
    return plan


def split(matrix):
    high = matrix.astype(BF16)
    low = (matrix - high.astype(np.float64)).astype(BF16)
    return high, low


def transforms():
    freq = (2.0 * np.pi / N) * (np.arange(HALF) + 0.5)[:, None]

    def forward(first, rows):
        angle = freq * (first + np.arange(rows))[None, :]
        return np.concatenate([np.cos(angle), -np.sin(angle)], axis=0)

    back = forward(0, SHORT).T * (2.0 / N)
    return split(forward(-ZLEAD, TRAIL)) + split(forward(0, TRAIL)) + split(back)


def dot(a, b):
    return jnp.dot(a, b, preferred_element_type=F32)


def chunks(rows, size=32):
    return [(start, min(size, rows - start)) for start in range(0, rows, size)]


def block_kernel(plan, cap, info, *refs):
    tails = refs[: len(plan)]
    heads = refs[len(plan) : 2 * len(plan)]
    refs = refs[2 * len(plan) :]
    (streams, dy_in, filt, fz_hi, fz_lo, fd_hi, fd_lo, g_hi, g_lo) = refs[:9]
    grads_out, sums_out = refs[9:11]
    refs = refs[11:]
    (kw, vw, qw, dyw, ks, vs, zs, dyl, dyl_own, zh, hh, dh, dho, p_hi, p_lo, yz, dm) = refs[:17]
    before = refs[17 : 17 + len(plan)]
    after = refs[17 + len(plan) : 17 + 2 * len(plan)]
    before_q = refs[17 + 2 * len(plan)]
    cols = streams.shape[-1]
    count = info[0]
    remaining = info[1]

    @pl.when(pl.program_id(0) == 0)
    def _():
        for at, (big, small) in enumerate(plan):
            base, live = info[2 + 4 * at], info[3 + 4 * at]
            col = lax.broadcasted_iota(jnp.int32, (LEAD, big), 1)
            row = lax.broadcasted_iota(jnp.int32, (LEAD, big), 0)
            hit = (row - LEAD == col - big - base) & (big - col <= live)
            before[at][...] = jnp.where(hit, 1.0, 0.0).astype(BF16)
            if small:
                col = lax.broadcasted_iota(jnp.int32, (16, 16), 1)
                row = lax.broadcasted_iota(jnp.int32, (16, 16), 0)
                hit = (row == col - base) & (16 - col <= live)
                before_q[at] = jnp.where(hit, 1.0, 0.0).astype(BF16)
            base, live = info[4 + 4 * at], info[5 + 4 * at]
            col = lax.broadcasted_iota(jnp.int32, (TRAIL, big), 1)
            row = lax.broadcasted_iota(jnp.int32, (TRAIL, big), 0)
            hit = (row == col + base) & (col < live)
            after[at][...] = jnp.where(hit, 1.0, 0.0).astype(BF16)

    with jax.named_scope("windows"):
        for which, window in ((0, kw), (1, vw)):
            lead = None
            trail = None
            for at, (big, small) in enumerate(plan):
                part = dot(before[at][...], tails[at][which * big : (which + 1) * big, :])
                lead = part if lead is None else lead + part
                if small:
                    first = 2 * big + which * 16
                    part = dot(after[at][:SHORT, :16], heads[at][first : first + 16, :])
                    trail = part if trail is None else trail + part
            window[:LEAD, :] = lead
            window[LEAD:, :] = trail
            for start, size in chunks(cap):
                row = lax.broadcasted_iota(jnp.int32, (size, 1), 0) + start
                own = streams[1 + which, 0, start : start + size, :].astype(F32)
                window[LEAD + start : LEAD + start + size, :] += jnp.where(row < count, own, 0.0)
        lead = None
        for at, (big, small) in enumerate(plan):
            if small:
                part = dot(before_q[at], tails[at][2 * big : 2 * big + 16, :])
                lead = part if lead is None else lead + part
        qw[:8, :] = lead[8:]
        for which, window, first in ((0, qw, 8), (1, dyw, 0)):
            trail = None
            for at, (big, small) in enumerate(plan):
                part = dot(after[at][...], heads[at][which * big : (which + 1) * big, :])
                trail = part if trail is None else trail + part
            window[first:, :] = trail
            for start, size in chunks(cap):
                row = lax.broadcasted_iota(jnp.int32, (size, 1), 0) + start
                source = streams[0, 0, start : start + size, :] if which == 0 else dy_in[0, start : start + size, :]
                window[first + start : first + start + size, :] += jnp.where(
                    row < count, source.astype(F32), 0.0
                )

    taps = filt[LTAP : LTAP + 32, :].astype(F32)

    def tap(stream, index):
        at = stream * STAP + index
        return taps[at : at + 1, :]

    def causal(window, stream, start, size):
        rows = window[start : start + size + 8, :]
        total = tap(stream, 0) * rows[8:, :]
        for index in range(1, STAP):
            total = total + tap(stream, index) * rows[8 - index : 8 - index + size, :]
        return total

    with jax.named_scope("short_forward"):
        for start, size in chunks(TRAIL):
            span = slice(start, start + size)
            keys = causal(kw, 1, start, size)
            values = causal(vw, 2, start, size)
            ks[span, :] = keys
            vs[span, :] = values
            zs[span, :] = (keys * values).astype(BF16)
        for start, size in chunks(TRAIL):
            span = slice(start, start + size)
            grad = (dyw[span, :] * causal(qw, 0, start, size)).astype(BF16)
            dyl[span, :] = grad
            if start < cap:
                row = lax.broadcasted_iota(jnp.int32, (size, 1), 0) + start
                dyl_own[span, :] = jnp.where(row < count, grad.astype(F32), 0.0).astype(BF16)

    with jax.named_scope("transforms"):
        long = filt[:LTAP, :]
        zh[...] = dot(fz_hi[...], zs[...]) + dot(fz_lo[...], zs[...])
        hh[...] = dot(fd_hi[:, :LTAP], long) + dot(fd_lo[:, :LTAP], long)
        dh[...] = dot(fd_hi[...], dyl[...]) + dot(fd_lo[...], dyl[...])
        dho[...] = dot(fd_hi[:, :cap], dyl_own[...]) + dot(fd_lo[:, :cap], dyl_own[...])

    def product(a, b, conjugate):
        for start, size in chunks(HALF, 16):
            real, imag = slice(start, start + size), slice(HALF + start, HALF + start + size)
            ar, ai, br, bi = a[real, :], a[imag, :], b[real, :], b[imag, :]
            if conjugate:
                cr, ci = ar * br + ai * bi, ai * br - ar * bi
            else:
                cr, ci = ar * br - ai * bi, ai * br + ar * bi
            for span, part in ((real, cr), (imag, ci)):
                high = part.astype(BF16)
                p_hi[span, :] = high
                p_lo[span, :] = (part - high.astype(F32)).astype(BF16)

    def inverse(rows):
        return (
            dot(g_hi[:rows, :], p_hi[...])
            + dot(g_lo[:rows, :], p_hi[...])
            + dot(g_hi[:rows, :], p_lo[...])
        )

    with jax.named_scope("long_filter_grad"):
        product(dho, zh, True)
        sums_out[:LTAP, :] = inverse(LTAP)

    with jax.named_scope("long_forward"):
        product(zh, hh, False)
        yz[...] = inverse(SHORT)
        for start, size in chunks(SHORT):
            span = slice(start, start + size)
            dm[0, span, :] = (dyw[span, :] * yz[span, :]).astype(BF16).astype(F32)

    with jax.named_scope("long_backward"):
        product(dh, hh, True)
        yz[...] = inverse(SHORT)
        for start, size in chunks(SHORT):
            span = slice(start, start + size)
            own = slice(ZLEAD + start, ZLEAD + start + size)
            row = lax.broadcasted_iota(jnp.int32, (size, 1), 0) + start
            grad = jnp.where(row < remaining, yz[span, :], 0.0)
            dm[1, span, :] = (grad * vs[own, :]).astype(BF16).astype(F32)
            dm[2, span, :] = (grad * ks[own, :]).astype(BF16).astype(F32)

    with jax.named_scope("short_backward"):
        for stream, window, lead in ((0, qw, 8), (1, kw, LEAD), (2, vw, LEAD)):
            partial = [jnp.zeros((8, cols), F32) for _ in range(STAP)]
            for start, size in chunks(cap):
                row = lax.broadcasted_iota(jnp.int32, (size, 1), 0) + start
                rows = dm[stream, start : start + size + 8, :]
                total = tap(stream, 0) * rows[:size, :]
                for index in range(1, STAP):
                    total = total + tap(stream, index) * rows[index : index + size, :]
                grads_out[stream, 0, start : start + size, :] = jnp.where(
                    row < count, total, 0.0
                ).astype(BF16)
                mine = jnp.where(row < count, rows[:size, :], 0.0)
                source = window[lead + start - 8 : lead + start + size, :]
                for index in range(STAP):
                    terms = mine * source[8 - index : 8 - index + size, :]
                    for at in range(0, size, 8):
                        partial[index] = partial[index] + terms[at : at + 8, :]
            for index in range(STAP):
                at = LTAP + stream * STAP + index
                sums_out[at : at + 1, :] = jnp.sum(partial[index], axis=0, keepdims=True)
        used = LTAP + 3 * STAP
        sums_out[used:, :] = jnp.zeros((GROWS - used, cols), F32)


def run_blocks(plan, info, tails, heads, streams, cotangent, filters, width=256):
    cap, channels = streams.shape[2:]
    width = min(width, channels)
    matrices = transforms()

    def by_block(rows):
        return pl.BlockSpec((rows, width), lambda step: (0, step))

    whole = [pl.BlockSpec(matrix.shape, lambda step: (0, 0)) for matrix in matrices]
    f32_rows = [
        LEAD + SHORT, LEAD + SHORT, 8 + TRAIL, TRAIL, TRAIL, TRAIL,
    ]
    scratch = [pltpu.VMEM((rows, width), F32) for rows in f32_rows]
    scratch += [pltpu.VMEM((rows, width), BF16) for rows in (TRAIL, TRAIL, cap)]
    scratch += [pltpu.VMEM((N, width), F32) for _ in range(4)]
    scratch += [pltpu.VMEM((N, width), BF16) for _ in range(2)]
    scratch += [pltpu.VMEM((SHORT, width), F32), pltpu.VMEM((3, SHORT, width), F32)]
    scratch += [pltpu.VMEM((LEAD, big), BF16) for big, _ in plan]
    scratch += [pltpu.VMEM((TRAIL, big), BF16) for big, _ in plan]
    scratch += [pltpu.VMEM((len(plan), 16, 16), BF16)]
    return pl.pallas_call(
        functools.partial(block_kernel, plan, cap),
        grid=(channels // width,),
        in_specs=[pl.BlockSpec(memory_space=pltpu.SMEM)]
        + [by_block(part.shape[0]) for part in tails + heads]
        + [
            pl.BlockSpec((3, 1, cap, width), lambda step: (0, 0, 0, step)),
            pl.BlockSpec((1, cap, width), lambda step: (0, 0, step)),
            by_block(filters.shape[0]),
        ]
        + whole,
        out_specs=[
            pl.BlockSpec((3, 1, cap, width), lambda step: (0, 0, 0, step)),
            by_block(GROWS),
        ],
        out_shape=[
            jax.ShapeDtypeStruct(streams.shape, BF16),
            jax.ShapeDtypeStruct((GROWS, channels), F32),
        ],
        scratch_shapes=scratch,
        compiler_params=pltpu.CompilerParams(vmem_limit_bytes=48 * 1024 * 1024),
        name="hyena_blocks",
    )(info, *tails, *heads, streams, cotangent, filters, *[jnp.asarray(m) for m in matrices])


def axis_copy(source, target, send_sem, recv_sem, axis, device):
    return pltpu.make_async_remote_copy(
        src_ref=source,
        dst_ref=target,
        send_sem=send_sem,
        recv_sem=recv_sem,
        device_id={axis: device},
        device_id_type=pl.DeviceIdType.MESH,
    )


def greet(axes):
    barrier = pltpu.get_barrier_semaphore()
    total = 0
    for axis in axes:
        size = lax.axis_size(axis)
        me = lax.axis_index(axis)
        for offset in range(1, size):
            pl.semaphore_signal(
                barrier,
                inc=1,
                device_id={axis: lax.rem(me + offset, size)},
                device_id_type=pl.DeviceIdType.MESH,
            )
        total += size - 1
    pl.semaphore_wait(barrier, total)


def exchange_kernel(plan, devices, count, kept, streams, cotangent, packed, *refs):
    tails = refs[: len(plan)]
    heads = refs[len(plan) : 2 * len(plan)]
    filters, last, zeros, send, recv, filter_send, filter_recv, own_sem, zero_sem = refs[2 * len(plan) :]
    me = lax.axis_index("ctx")
    cap, channels = kept.shape[2:]
    share = packed.shape[1]
    widest = plan[0][0]
    gather = filters.shape[1] > share
    mine = filters.at[:, pl.ds(pl.multiple_of(me * share, share), share)] if gather else filters
    own = pltpu.make_async_copy(packed, mine, own_sem)
    own.start()
    zeros[...] = jnp.zeros_like(zeros)

    head_copies, tail_copies, blanks = [], [], []
    slot = 0
    for at, (big, small) in enumerate(plan):
        distance = at + 1
        after = jnp.minimum(me + distance, devices - 1)
        before = jnp.maximum(me - distance, 0)
        pieces = [
            (streams.at[0, 0, pl.ds(0, big), :], 0, big),
            (cotangent.at[0, pl.ds(0, big), :], big, big),
        ]
        if small:
            pieces += [
                (streams.at[1, 0, pl.ds(0, small), :], 2 * big, small),
                (streams.at[2, 0, pl.ds(0, small), :], 2 * big + small, small),
            ]
        for source, first, rows in pieces:
            target = heads[at].at[pl.ds(first, rows), :]
            copy = axis_copy(source, target, send.at[slot], recv.at[slot], "ctx", before)
            head_copies.append((distance, copy))
            slot += 1
        if big == widest and small:
            pieces = [(last, 0, 2 * widest + small)]
        else:
            pieces = [
                (last.at[pl.ds(widest - big, big), :], 0, big),
                (last.at[pl.ds(2 * widest - big, big), :], big, big),
            ]
            if small:
                pieces.append((last.at[pl.ds(2 * widest, small), :], 2 * big, small))
        for source, first, rows in pieces:
            target = tails[at].at[pl.ds(first, rows), :]
            copy = axis_copy(source, target, send.at[slot], recv.at[slot], "ctx", after)
            tail_copies.append((distance, copy))
            slot += 1
        rows = tails[at].shape[0]
        blank = pltpu.make_async_copy(zeros.at[pl.ds(0, rows), :], tails[at], zero_sem.at[2 * at])
        blanks.append((me < distance, blank))
        rows = heads[at].shape[0]
        blank = pltpu.make_async_copy(zeros.at[pl.ds(0, rows), :], heads[at], zero_sem.at[2 * at + 1])
        blanks.append((me + distance >= devices, blank))

    filter_copies = []
    for offset in range(1, devices if gather else 1):
        peer = lax.rem(me + offset, devices)
        filter_copies.append(
            axis_copy(packed, mine, filter_send.at[offset], filter_recv.at[offset], "ctx", peer)
        )

    for missing, blank in blanks:
        pl.when(missing)(blank.start)
    greet(("ctx",))
    for distance, copy in head_copies:
        pl.when(me >= distance)(copy.start)
    live = count[0, 0]
    col = lax.broadcasted_iota(jnp.int32, (widest, cap), 1)
    row = lax.broadcasted_iota(jnp.int32, (widest, cap), 0)
    pick = jnp.where(col - row == live - widest, 1.0, 0.0).astype(BF16)
    width = min(512, channels)
    for start in range(0, channels, width):
        span = slice(start, start + width)
        last[:widest, span] = dot(pick, kept[1, 0, :, span]).astype(BF16)
        last[widest : 2 * widest, span] = dot(pick, kept[2, 0, :, span]).astype(BF16)
        last[2 * widest :, span] = dot(pick[widest - 16 :], kept[0, 0, :, span]).astype(BF16)
    for distance, copy in tail_copies:
        pl.when(me + distance < devices)(copy.start)
    for copy in filter_copies:
        copy.start()
    for missing, blank in blanks:
        pl.when(missing)(blank.wait)
    own.wait()
    for distance, copy in head_copies:
        pl.when(me >= distance)(copy.wait_send)
        pl.when(me + distance < devices)(copy.wait_recv)
    for distance, copy in tail_copies:
        pl.when(me + distance < devices)(copy.wait_send)
        pl.when(me >= distance)(copy.wait_recv)
    for copy in filter_copies:
        copy.wait_send()
        copy.wait_recv()


def exchange(plan, devices, streams, cotangent, counts, packed):
    channels = streams.shape[3]
    width = packed.shape[1] * (devices if packed.shape[1] % 128 == 0 else 1)
    tails = [2 * big + small for big, small in plan]
    heads = [2 * big + 2 * small for big, small in plan]
    copies = 8 * len(plan)
    out = pl.pallas_call(
        functools.partial(exchange_kernel, plan, devices),
        in_specs=[
            pl.BlockSpec(memory_space=pltpu.SMEM),
            pl.BlockSpec(memory_space=pltpu.VMEM),
        ]
        + [pl.BlockSpec(memory_space=pl.ANY)] * 3,
        out_specs=[pl.BlockSpec(memory_space=pl.ANY)] * (2 * len(plan) + 1),
        out_shape=[jax.ShapeDtypeStruct((rows, channels), BF16) for rows in tails + heads]
        + [jax.ShapeDtypeStruct((packed.shape[0], width), BF16)],
        scratch_shapes=[
            pltpu.VMEM((2 * plan[0][0] + 16, channels), BF16),
            pltpu.VMEM((max(heads), channels), BF16),
            pltpu.SemaphoreType.DMA((copies,)),
            pltpu.SemaphoreType.DMA((copies,)),
            pltpu.SemaphoreType.DMA((devices,)),
            pltpu.SemaphoreType.DMA((devices,)),
            pltpu.SemaphoreType.DMA,
            pltpu.SemaphoreType.DMA((2 * len(plan),)),
        ],
        compiler_params=pltpu.CompilerParams(
            collective_id=0, has_side_effects=True, vmem_limit_bytes=32 * 1024 * 1024
        ),
        name="exchange",
    )(counts, streams, streams, cotangent, packed)
    return out[: len(plan)], out[len(plan) : 2 * len(plan)], out[2 * len(plan)]


def reduce_kernel(
    devices, groups, sums, long_out, short_out,
    outgoing, incoming, total, dp_parts, ctx_parts, send, recv, dp_send, dp_recv, ctx_send, ctx_recv,
):
    me = lax.axis_index("ctx")
    group = lax.axis_index("dp")
    share = long_out.shape[1]

    def columns(device):
        return pl.ds(pl.multiple_of(device * share, share), share)

    greet(("ctx", "dp"))
    copies = []
    for offset in range(1, devices):
        peer = lax.rem(me + offset, devices)
        outgoing[offset] = sums[:, columns(peer)].astype(BF16)
        copy = axis_copy(
            outgoing.at[offset], incoming.at[offset], send.at[offset], recv.at[offset], "ctx", peer
        )
        copy.start()
        copies.append(copy)
    total[...] = sums[:, columns(me)]
    for offset in range(1, devices):
        copies[offset - 1].wait_recv()
        total[...] += incoming[offset].astype(F32)
    squares = jnp.zeros((8, 128), F32)
    for row in range(0, GROWS, 8):
        for col in range(0, share, 128):
            part = total[row : row + 8, col : col + 128]
            squares = squares + part * part
    for axis, size, mine, parts, out_sem, in_sem in (
        ("dp", groups, group, dp_parts, dp_send, dp_recv),
        ("ctx", devices, me, ctx_parts, ctx_send, ctx_recv),
    ):
        parts[0] = squares
        for offset in range(1, size):
            copy = axis_copy(
                parts.at[0], parts.at[offset], out_sem.at[offset], in_sem.at[offset],
                axis, lax.rem(mine + offset, size),
            )
            copy.start()
            copies.append(copy)
        for offset in range(1, size):
            copies[offset - size].wait_recv()
            squares = squares + parts[offset]
    for copy in copies:
        copy.wait_send()
    whole = jnp.sum(jnp.sum(squares, axis=0, keepdims=True), axis=1, keepdims=True)
    rms = jnp.sqrt(whole / float((LTAP + 3 * STAP) * CH) + 1e-06)
    long_out[...] = total[:LTAP, :] / rms
    short_out[...] = total[LTAP:, :] / rms


def reduce_sums(sums, devices, groups):
    share = sums.shape[1] // devices
    dma = pltpu.SemaphoreType.DMA
    return pl.pallas_call(
        functools.partial(reduce_kernel, devices, groups),
        in_specs=[pl.BlockSpec(memory_space=pltpu.VMEM)],
        out_specs=[pl.BlockSpec(memory_space=pltpu.VMEM)] * 2,
        out_shape=[
            jax.ShapeDtypeStruct((LTAP, share), F32),
            jax.ShapeDtypeStruct((GROWS - LTAP, share), F32),
        ],
        scratch_shapes=[
            pltpu.VMEM((devices, GROWS, share), BF16),
            pltpu.VMEM((devices, GROWS, share), BF16),
            pltpu.VMEM((GROWS, share), F32),
            pltpu.VMEM((groups, 8, 128), F32),
            pltpu.VMEM((devices, 8, 128), F32),
            dma((devices,)),
            dma((devices,)),
            dma((groups,)),
            dma((groups,)),
            dma((devices,)),
            dma((devices,)),
        ],
        compiler_params=pltpu.CompilerParams(
            collective_id=1, has_side_effects=True, vmem_limit_bytes=32 * 1024 * 1024
        ),
        name="reduce_sums",
    )(sums)


def halo_info(counts, me, plan):
    ids = jnp.arange(counts.shape[0], dtype=jnp.int32)
    spans = [(0, 1), (0, counts.shape[0])]
    for distance in range(1, len(plan) + 1):
        spans += [(1 - distance, 0), (-distance, 1 - distance), (0, distance), (distance, distance + 1)]
    spans = np.asarray(spans, np.int32)
    at = ids[None, :] - me
    inside = (at >= spans[:, :1]) & (at < spans[:, 1:])
    return jnp.sum(jnp.where(inside, counts[None, :], 0), axis=1)


def local(streams, cotangent, counts, short_filters, long_filter):
    devices = lax.axis_size("ctx")
    me = lax.axis_index("ctx")
    live_count = counts[0, 0]
    share = long_filter.shape[1]
    plan = halo_plan(devices, streams.shape[2])
    digits = jnp.stack([live_count // 16, live_count % 16]).astype(BF16)
    packed = jnp.concatenate(
        [
            long_filter,
            short_filters.reshape(3 * STAP, share),
            jnp.broadcast_to(digits[:, None], (2, share)),
            jnp.zeros((160 - LTAP - 3 * STAP - 2, share), BF16),
        ],
        axis=0,
    )
    tails, heads, filters = exchange(plan, devices, streams, cotangent, counts, packed)
    if share % 128:
        filters = lax.all_gather(packed, "ctx", axis=1, tiled=True)
    digits = filters[LTAP + 3 * STAP : LTAP + 3 * STAP + 2, ::share].astype(jnp.int32)
    info = halo_info(digits[0] * 16 + digits[1], me, plan)
    stream_grads, sums = run_blocks(plan, info, tails, heads, streams, cotangent, filters)
    if share % 128:
        own = lax.psum_scatter(sums, "ctx", scatter_dimension=1, tiled=True)
        squares = lax.psum(jnp.sum(own * own), ("dp", "ctx"))
        own = own / jnp.sqrt(squares / float((LTAP + 3 * STAP) * CH) + 1e-06)
        long_grad, short_rows = own[:LTAP], own[LTAP:]
    else:
        long_grad, short_rows = reduce_sums(sums, devices, lax.axis_size("dp"))
    short_grad = short_rows[: 3 * STAP].reshape(3, STAP, share)
    return (stream_grads, long_grad, short_grad)


def solution(mesh):
    return jax.shard_map(
        local,
        mesh=mesh,
        in_specs=(
            P(None, None, "ctx", "dp"),
            P(None, "ctx", "dp"),
            P(None, "ctx"),
            P(None, None, ("dp", "ctx")),
            P(None, ("dp", "ctx")),
        ),
        out_specs=(
            P(None, None, "ctx", "dp"),
            P(None, ("dp", "ctx")),
            P(None, None, ("dp", "ctx")),
        ),
        check_vma=False,
    )
```

```python
import functools

import jax
import jax.numpy as jnp
import numpy as np
from jax import lax
from jax.experimental import pallas as pl
from jax.experimental.pallas import tpu as pltpu
from jax.sharding import PartitionSpec as P

CH = 8192
LTAP = 128
STAP = 7
MEAN_COUNT = 256
REACH = LTAP - 1 + STAP - 1
N = 480
HALF = N // 2
LEAD = 136
TRAIL = 464
SHORT = 336
ZLEAD = 128
GROWS = 160
F32 = jnp.float32
BF16 = jnp.bfloat16


def ceil16(rows):
    return -(-rows // 16) * 16


def halo_plan(devices, cap):
    slack = devices * cap - devices * MEAN_COUNT
    plan = []
    for distance in range(1, devices):
        nearer = max(distance - 1, (distance - 1) * cap - slack)
        if nearer >= REACH:
            break
        big = ceil16(REACH - nearer)
        small = 16 if nearer < STAP - 1 else 0
        plan.append((big, small))
    return plan


def split(matrix):
    high = matrix.astype(BF16)
    low = (matrix - high.astype(np.float64)).astype(BF16)
    return high, low


def transforms():
    freq = (2.0 * np.pi / N) * (np.arange(HALF) + 0.5)[:, None]

    def forward(first, rows):
        angle = freq * (first + np.arange(rows))[None, :]
        return np.concatenate([np.cos(angle), -np.sin(angle)], axis=0)

    back = forward(0, SHORT).T * (2.0 / N)
    return split(forward(-ZLEAD, TRAIL)) + split(forward(0, TRAIL)) + split(back)


def dot(a, b):
    return jnp.dot(a, b, preferred_element_type=F32)


def chunks(rows, size=32):
    return [(start, min(size, rows - start)) for start in range(0, rows, size)]


def block_kernel(plan, cap, info, *refs):
    tails = refs[: len(plan)]
    heads = refs[len(plan) : 2 * len(plan)]
    refs = refs[2 * len(plan) :]
    (streams, dy_in, filt, fz_hi, fz_lo, fd_hi, fd_lo, g_hi, g_lo) = refs[:9]
    grads_out, sums_out = refs[9:11]
    refs = refs[11:]
    (kw, vw, qw, dyw, ks, vs, zs, dyl, dyl_own, zh, hh, dh, dho, p_hi, p_lo, yz, dm) = refs[:17]
    before = refs[17 : 17 + len(plan)]
    after = refs[17 + len(plan) : 17 + 2 * len(plan)]
    before_q = refs[17 + 2 * len(plan)]
    cols = streams.shape[-1]
    count = info[0]
    remaining = info[1]

    @pl.when(pl.program_id(0) == 0)
    def _():
        for at, (big, small) in enumerate(plan):
            base, live = info[2 + 4 * at], info[3 + 4 * at]
            col = lax.broadcasted_iota(jnp.int32, (LEAD, big), 1)
            row = lax.broadcasted_iota(jnp.int32, (LEAD, big), 0)
            hit = (row - LEAD == col - big - base) & (big - col <= live)
            before[at][...] = jnp.where(hit, 1.0, 0.0).astype(BF16)
            if small:
                col = lax.broadcasted_iota(jnp.int32, (16, 16), 1)
                row = lax.broadcasted_iota(jnp.int32, (16, 16), 0)
                hit = (row == col - base) & (16 - col <= live)
                before_q[at] = jnp.where(hit, 1.0, 0.0).astype(BF16)
            base, live = info[4 + 4 * at], info[5 + 4 * at]
            col = lax.broadcasted_iota(jnp.int32, (TRAIL, big), 1)
            row = lax.broadcasted_iota(jnp.int32, (TRAIL, big), 0)
            hit = (row == col + base) & (col < live)
            after[at][...] = jnp.where(hit, 1.0, 0.0).astype(BF16)

    with jax.named_scope("windows"):
        for which, window in ((0, kw), (1, vw)):
            lead = None
            trail = None
            for at, (big, small) in enumerate(plan):
                part = dot(before[at][...], tails[at][which * big : (which + 1) * big, :])
                lead = part if lead is None else lead + part
                if small:
                    first = 2 * big + which * 16
                    part = dot(after[at][:SHORT, :16], heads[at][first : first + 16, :])
                    trail = part if trail is None else trail + part
            window[:LEAD, :] = lead
            window[LEAD:, :] = trail
            for start, size in chunks(cap):
                row = lax.broadcasted_iota(jnp.int32, (size, 1), 0) + start
                own = streams[1 + which, 0, start : start + size, :].astype(F32)
                window[LEAD + start : LEAD + start + size, :] += jnp.where(row < count, own, 0.0)
        lead = None
        for at, (big, small) in enumerate(plan):
            if small:
                part = dot(before_q[at], tails[at][2 * big : 2 * big + 16, :])
                lead = part if lead is None else lead + part
        qw[:8, :] = lead[8:]
        for which, window, first in ((0, qw, 8), (1, dyw, 0)):
            trail = None
            for at, (big, small) in enumerate(plan):
                part = dot(after[at][...], heads[at][which * big : (which + 1) * big, :])
                trail = part if trail is None else trail + part
            window[first:, :] = trail
            for start, size in chunks(cap):
                row = lax.broadcasted_iota(jnp.int32, (size, 1), 0) + start
                source = streams[0, 0, start : start + size, :] if which == 0 else dy_in[0, start : start + size, :]
                window[first + start : first + start + size, :] += jnp.where(
                    row < count, source.astype(F32), 0.0
                )

    taps = filt[LTAP : LTAP + 32, :].astype(F32)

    def tap(stream, index):
        at = stream * STAP + index
        return taps[at : at + 1, :]

    def causal(window, stream, start, size):
        rows = window[start : start + size + 8, :]
        total = tap(stream, 0) * rows[8:, :]
        for index in range(1, STAP):
            total = total + tap(stream, index) * rows[8 - index : 8 - index + size, :]
        return total

    with jax.named_scope("short_forward"):
        for start, size in chunks(TRAIL):
            span = slice(start, start + size)
            keys = causal(kw, 1, start, size)
            values = causal(vw, 2, start, size)
            ks[span, :] = keys
            vs[span, :] = values
            zs[span, :] = (keys * values).astype(BF16)
        for start, size in chunks(TRAIL):
            span = slice(start, start + size)
            grad = (dyw[span, :] * causal(qw, 0, start, size)).astype(BF16)
            dyl[span, :] = grad
            if start < cap:
                row = lax.broadcasted_iota(jnp.int32, (size, 1), 0) + start
                dyl_own[span, :] = jnp.where(row < count, grad.astype(F32), 0.0).astype(BF16)

    with jax.named_scope("transforms"):
        long = filt[:LTAP, :]
        zh[...] = dot(fz_hi[...], zs[...]) + dot(fz_lo[...], zs[...])
        hh[...] = dot(fd_hi[:, :LTAP], long) + dot(fd_lo[:, :LTAP], long)
        dh[...] = dot(fd_hi[...], dyl[...]) + dot(fd_lo[...], dyl[...])
        dho[...] = dot(fd_hi[:, :cap], dyl_own[...]) + dot(fd_lo[:, :cap], dyl_own[...])

    def product(a, b, conjugate):
        for start, size in chunks(HALF, 16):
            real, imag = slice(start, start + size), slice(HALF + start, HALF + start + size)
            ar, ai, br, bi = a[real, :], a[imag, :], b[real, :], b[imag, :]
            if conjugate:
                cr, ci = ar * br + ai * bi, ai * br - ar * bi
            else:
                cr, ci = ar * br - ai * bi, ai * br + ar * bi
            for span, part in ((real, cr), (imag, ci)):
                high = part.astype(BF16)
                p_hi[span, :] = high
                p_lo[span, :] = (part - high.astype(F32)).astype(BF16)

    def inverse(rows):
        return (
            dot(g_hi[:rows, :], p_hi[...])
            + dot(g_lo[:rows, :], p_hi[...])
            + dot(g_hi[:rows, :], p_lo[...])
        )

    with jax.named_scope("long_filter_grad"):
        product(dho, zh, True)
        sums_out[:LTAP, :] = inverse(LTAP)

    with jax.named_scope("long_forward"):
        product(zh, hh, False)
        yz[...] = inverse(SHORT)
        for start, size in chunks(SHORT):
            span = slice(start, start + size)
            dm[0, span, :] = (dyw[span, :] * yz[span, :]).astype(BF16).astype(F32)

    with jax.named_scope("long_backward"):
        product(dh, hh, True)
        yz[...] = inverse(SHORT)
        for start, size in chunks(SHORT):
            span = slice(start, start + size)
            own = slice(ZLEAD + start, ZLEAD + start + size)
            row = lax.broadcasted_iota(jnp.int32, (size, 1), 0) + start
            grad = jnp.where(row < remaining, yz[span, :], 0.0)
            dm[1, span, :] = (grad * vs[own, :]).astype(BF16).astype(F32)
            dm[2, span, :] = (grad * ks[own, :]).astype(BF16).astype(F32)

    with jax.named_scope("short_backward"):
        for stream, window, lead in ((0, qw, 8), (1, kw, LEAD), (2, vw, LEAD)):
            partial = [jnp.zeros((8, cols), F32) for _ in range(STAP)]
            for start, size in chunks(cap):
                row = lax.broadcasted_iota(jnp.int32, (size, 1), 0) + start
                rows = dm[stream, start : start + size + 8, :]
                total = tap(stream, 0) * rows[:size, :]
                for index in range(1, STAP):
                    total = total + tap(stream, index) * rows[index : index + size, :]
                grads_out[stream, 0, start : start + size, :] = jnp.where(
                    row < count, total, 0.0
                ).astype(BF16)
                mine = jnp.where(row < count, rows[:size, :], 0.0)
                source = window[lead + start - 8 : lead + start + size, :]
                for index in range(STAP):
                    terms = mine * source[8 - index : 8 - index + size, :]
                    for at in range(0, size, 8):
                        partial[index] = partial[index] + terms[at : at + 8, :]
            for index in range(STAP):
                at = LTAP + stream * STAP + index
                sums_out[at : at + 1, :] = jnp.sum(partial[index], axis=0, keepdims=True)
        used = LTAP + 3 * STAP
        sums_out[used:, :] = jnp.zeros((GROWS - used, cols), F32)


def run_blocks(plan, info, tails, heads, streams, cotangent, filters, width=256):
    cap, channels = streams.shape[2:]
    width = min(width, channels)
    matrices = transforms()

    def by_block(rows):
        return pl.BlockSpec((rows, width), lambda step: (0, step))

    whole = [pl.BlockSpec(matrix.shape, lambda step: (0, 0)) for matrix in matrices]
    f32_rows = [
        LEAD + SHORT, LEAD + SHORT, 8 + TRAIL, TRAIL, TRAIL, TRAIL,
    ]
    scratch = [pltpu.VMEM((rows, width), F32) for rows in f32_rows]
    scratch += [pltpu.VMEM((rows, width), BF16) for rows in (TRAIL, TRAIL, cap)]
    scratch += [pltpu.VMEM((N, width), F32) for _ in range(4)]
    scratch += [pltpu.VMEM((N, width), BF16) for _ in range(2)]
    scratch += [pltpu.VMEM((SHORT, width), F32), pltpu.VMEM((3, SHORT, width), F32)]
    scratch += [pltpu.VMEM((LEAD, big), BF16) for big, _ in plan]
    scratch += [pltpu.VMEM((TRAIL, big), BF16) for big, _ in plan]
    scratch += [pltpu.VMEM((len(plan), 16, 16), BF16)]
    return pl.pallas_call(
        functools.partial(block_kernel, plan, cap),
        grid=(channels // width,),
        in_specs=[pl.BlockSpec(memory_space=pltpu.SMEM)]
        + [by_block(part.shape[0]) for part in tails + heads]
        + [
            pl.BlockSpec((3, 1, cap, width), lambda step: (0, 0, 0, step)),
            pl.BlockSpec((1, cap, width), lambda step: (0, 0, step)),
            by_block(filters.shape[0]),
        ]
        + whole,
        out_specs=[
            pl.BlockSpec((3, 1, cap, width), lambda step: (0, 0, 0, step)),
            by_block(GROWS),
        ],
        out_shape=[
            jax.ShapeDtypeStruct(streams.shape, BF16),
            jax.ShapeDtypeStruct((GROWS, channels), F32),
        ],
        scratch_shapes=scratch,
        compiler_params=pltpu.CompilerParams(vmem_limit_bytes=60 * 1024 * 1024),
        name="hyena_blocks",
    )(info, *tails, *heads, streams, cotangent, filters, *[jnp.asarray(m) for m in matrices])


def axis_copy(source, target, send_sem, recv_sem, axis, device):
    return pltpu.make_async_remote_copy(
        src_ref=source,
        dst_ref=target,
        send_sem=send_sem,
        recv_sem=recv_sem,
        device_id={axis: device},
        device_id_type=pl.DeviceIdType.MESH,
    )


def greet(axes):
    barrier = pltpu.get_barrier_semaphore()
    total = 0
    for axis in axes:
        size = lax.axis_size(axis)
        me = lax.axis_index(axis)
        for offset in range(1, size):
            pl.semaphore_signal(
                barrier,
                inc=1,
                device_id={axis: lax.rem(me + offset, size)},
                device_id_type=pl.DeviceIdType.MESH,
            )
        total += size - 1
    pl.semaphore_wait(barrier, total)


def exchange_kernel(plan, devices, count, kept, streams, cotangent, packed, *refs):
    tails = refs[: len(plan)]
    heads = refs[len(plan) : 2 * len(plan)]
    filters, last, zeros, send, recv, filter_send, filter_recv, own_sem, zero_sem = refs[2 * len(plan) :]
    me = lax.axis_index("ctx")
    cap, channels = kept.shape[2:]
    share = packed.shape[1]
    widest = plan[0][0]
    gather = filters.shape[1] > share
    mine = filters.at[:, pl.ds(pl.multiple_of(me * share, share), share)] if gather else filters
    own = pltpu.make_async_copy(packed, mine, own_sem)
    own.start()
    zeros[...] = jnp.zeros_like(zeros)

    relayed = len(plan) > 1 and plan[0] == plan[1]
    even = lax.rem(me, 2) == 0
    odd = lax.rem(me, 2) == 1
    head_relays, tail_relays = [], []
    head_copies, tail_copies, blanks = [], [], []
    slot = 0
    for at, (big, small) in enumerate(plan):
        distance = at + 1
        after = jnp.minimum(me + distance, devices - 1)
        before = jnp.maximum(me - distance, 0)
        pieces = [
            (streams.at[0, 0, pl.ds(0, big), :], 0, big),
            (cotangent.at[0, pl.ds(0, big), :], big, big),
        ]
        if small:
            pieces += [
                (streams.at[1, 0, pl.ds(0, small), :], 2 * big, small),
                (streams.at[2, 0, pl.ds(0, small), :], 2 * big + small, small),
            ]
        for source, first, rows in pieces:
            target = heads[at].at[pl.ds(first, rows), :]
            copy = axis_copy(source, target, send.at[slot], recv.at[slot], "ctx", before)
            head_copies.append((distance, copy))
            slot += 1
            if relayed and at == 1:
                passed = heads[0].at[pl.ds(first, rows), :]
                head_relays.append(
                    axis_copy(passed, target, send.at[slot], recv.at[slot - 1], "ctx", jnp.maximum(me - 1, 0))
                )
                slot += 1
        if big == widest and small:
            pieces = [(last, 0, 2 * widest + small)]
        else:
            pieces = [
                (last.at[pl.ds(widest - big, big), :], 0, big),
                (last.at[pl.ds(2 * widest - big, big), :], big, big),
            ]
            if small:
                pieces.append((last.at[pl.ds(2 * widest, small), :], 2 * big, small))
        for source, first, rows in pieces:
            target = tails[at].at[pl.ds(first, rows), :]
            copy = axis_copy(source, target, send.at[slot], recv.at[slot], "ctx", after)
            tail_copies.append((distance, copy))
            slot += 1
            if relayed and at == 1:
                passed = tails[0].at[pl.ds(first, rows), :]
                tail_relays.append(
                    axis_copy(
                        passed, target, send.at[slot], recv.at[slot - 1], "ctx", jnp.minimum(me + 1, devices - 1)
                    )
                )
                slot += 1
        rows = tails[at].shape[0]
        blank = pltpu.make_async_copy(zeros.at[pl.ds(0, rows), :], tails[at], zero_sem.at[2 * at])
        blanks.append((me < distance, blank))
        rows = heads[at].shape[0]
        blank = pltpu.make_async_copy(zeros.at[pl.ds(0, rows), :], heads[at], zero_sem.at[2 * at + 1])
        blanks.append((me + distance >= devices, blank))

    filter_copies = []
    for offset in range(1, devices if gather else 1):
        peer = lax.rem(me + offset, devices)
        filter_copies.append(
            axis_copy(packed, mine, filter_send.at[offset], filter_recv.at[offset], "ctx", peer)
        )

    for missing, blank in blanks:
        pl.when(missing)(blank.start)
    greet(("ctx",))
    def sends_head(distance):
        return (me >= distance) & odd if relayed and distance == 2 else me >= distance

    def sends_tail(distance):
        fits = me + distance < devices
        return fits & even if relayed and distance == 2 else fits

    for distance, copy in head_copies:
        pl.when(sends_head(distance))(copy.start)
    live = count[0, 0]
    col = lax.broadcasted_iota(jnp.int32, (widest, cap), 1)
    row = lax.broadcasted_iota(jnp.int32, (widest, cap), 0)
    pick = jnp.where(col - row == live - widest, 1.0, 0.0).astype(BF16)
    width = min(512, channels)
    for start in range(0, channels, width):
        span = slice(start, start + width)
        last[:widest, span] = dot(pick, kept[1, 0, :, span]).astype(BF16)
        last[widest : 2 * widest, span] = dot(pick, kept[2, 0, :, span]).astype(BF16)
        last[2 * widest :, span] = dot(pick[widest - 16 :], kept[0, 0, :, span]).astype(BF16)
    for distance, copy in tail_copies:
        pl.when(sends_tail(distance))(copy.start)
    for copy in filter_copies:
        copy.start()
    for missing, blank in blanks:
        pl.when(missing)(blank.wait)
    own.wait()
    pass_head = odd & (me + 1 < devices)
    pass_tail = even & (me >= 1) & (me + 1 < devices)
    for distance, copy in head_copies:
        if distance == 1:
            pl.when(me + 1 < devices)(copy.wait_recv)
    for copy in head_relays:
        pl.when(pass_head)(copy.start)
    for distance, copy in tail_copies:
        if distance == 1:
            pl.when(me >= 1)(copy.wait_recv)
    for copy in tail_relays:
        pl.when(pass_tail)(copy.start)
    for distance, copy in head_copies:
        pl.when(sends_head(distance))(copy.wait_send)
        if distance > 1:
            pl.when(me + distance < devices)(copy.wait_recv)
    for distance, copy in tail_copies:
        pl.when(sends_tail(distance))(copy.wait_send)
        if distance > 1:
            pl.when(me >= distance)(copy.wait_recv)
    for copy in head_relays:
        pl.when(pass_head)(copy.wait_send)
    for copy in tail_relays:
        pl.when(pass_tail)(copy.wait_send)
    for copy in filter_copies:
        copy.wait_send()
        copy.wait_recv()


def exchange(plan, devices, streams, cotangent, counts, packed):
    channels = streams.shape[3]
    width = packed.shape[1] * (devices if packed.shape[1] % 128 == 0 else 1)
    tails = [2 * big + small for big, small in plan]
    heads = [2 * big + 2 * small for big, small in plan]
    copies = 8 * len(plan)
    out = pl.pallas_call(
        functools.partial(exchange_kernel, plan, devices),
        in_specs=[
            pl.BlockSpec(memory_space=pltpu.SMEM),
            pl.BlockSpec(memory_space=pltpu.VMEM),
        ]
        + [pl.BlockSpec(memory_space=pl.ANY)] * 3,
        out_specs=[pl.BlockSpec(memory_space=pl.ANY)] * (2 * len(plan) + 1),
        out_shape=[jax.ShapeDtypeStruct((rows, channels), BF16) for rows in tails + heads]
        + [jax.ShapeDtypeStruct((packed.shape[0], width), BF16)],
        scratch_shapes=[
            pltpu.VMEM((2 * plan[0][0] + 16, channels), BF16),
            pltpu.VMEM((max(heads), channels), BF16),
            pltpu.SemaphoreType.DMA((copies,)),
            pltpu.SemaphoreType.DMA((copies,)),
            pltpu.SemaphoreType.DMA((devices,)),
            pltpu.SemaphoreType.DMA((devices,)),
            pltpu.SemaphoreType.DMA,
            pltpu.SemaphoreType.DMA((2 * len(plan),)),
        ],
        compiler_params=pltpu.CompilerParams(
            collective_id=0, has_side_effects=True, vmem_limit_bytes=32 * 1024 * 1024
        ),
        name="exchange",
    )(counts, streams, streams, cotangent, packed)
    return out[: len(plan)], out[len(plan) : 2 * len(plan)], out[2 * len(plan)]


def reduce_kernel(
    devices, groups, sums, long_out, short_out,
    outgoing, incoming, total, dp_parts, ctx_parts, send, recv, dp_send, dp_recv, ctx_send, ctx_recv,
):
    me = lax.axis_index("ctx")
    group = lax.axis_index("dp")
    share = long_out.shape[1]

    def columns(device):
        return pl.ds(pl.multiple_of(device * share, share), share)

    greet(("ctx", "dp"))
    copies = []
    for offset in range(1, devices):
        peer = lax.rem(me + offset, devices)
        outgoing[offset] = sums[:, columns(peer)].astype(BF16)
        copy = axis_copy(
            outgoing.at[offset], incoming.at[offset], send.at[offset], recv.at[offset], "ctx", peer
        )
        copy.start()
        copies.append(copy)
    total[...] = sums[:, columns(me)]
    for offset in range(1, devices):
        copies[offset - 1].wait_recv()
        total[...] += incoming[offset].astype(F32)
    squares = jnp.zeros((8, 128), F32)
    for row in range(0, GROWS, 8):
        for col in range(0, share, 128):
            part = total[row : row + 8, col : col + 128]
            squares = squares + part * part
    for axis, size, mine, parts, out_sem, in_sem in (
        ("dp", groups, group, dp_parts, dp_send, dp_recv),
        ("ctx", devices, me, ctx_parts, ctx_send, ctx_recv),
    ):
        parts[0] = squares
        for offset in range(1, size):
            copy = axis_copy(
                parts.at[0], parts.at[offset], out_sem.at[offset], in_sem.at[offset],
                axis, lax.rem(mine + offset, size),
            )
            copy.start()
            copies.append(copy)
        for offset in range(1, size):
            copies[offset - size].wait_recv()
            squares = squares + parts[offset]
    for copy in copies:
        copy.wait_send()
    whole = jnp.sum(jnp.sum(squares, axis=0, keepdims=True), axis=1, keepdims=True)
    rms = jnp.sqrt(whole / float((LTAP + 3 * STAP) * CH) + 1e-06)
    long_out[...] = total[:LTAP, :] / rms
    short_out[...] = total[LTAP:, :] / rms


def reduce_sums(sums, devices, groups):
    share = sums.shape[1] // devices
    dma = pltpu.SemaphoreType.DMA
    return pl.pallas_call(
        functools.partial(reduce_kernel, devices, groups),
        in_specs=[pl.BlockSpec(memory_space=pltpu.VMEM)],
        out_specs=[pl.BlockSpec(memory_space=pltpu.VMEM)] * 2,
        out_shape=[
            jax.ShapeDtypeStruct((LTAP, share), F32),
            jax.ShapeDtypeStruct((GROWS - LTAP, share), F32),
        ],
        scratch_shapes=[
            pltpu.VMEM((devices, GROWS, share), BF16),
            pltpu.VMEM((devices, GROWS, share), BF16),
            pltpu.VMEM((GROWS, share), F32),
            pltpu.VMEM((groups, 8, 128), F32),
            pltpu.VMEM((devices, 8, 128), F32),
            dma((devices,)),
            dma((devices,)),
            dma((groups,)),
            dma((groups,)),
            dma((devices,)),
            dma((devices,)),
        ],
        compiler_params=pltpu.CompilerParams(
            collective_id=1, has_side_effects=True, vmem_limit_bytes=32 * 1024 * 1024
        ),
        name="reduce_sums",
    )(sums)


def halo_info(counts, me, plan):
    ids = jnp.arange(counts.shape[0], dtype=jnp.int32)
    spans = [(0, 1), (0, counts.shape[0])]
    for distance in range(1, len(plan) + 1):
        spans += [(1 - distance, 0), (-distance, 1 - distance), (0, distance), (distance, distance + 1)]
    spans = np.asarray(spans, np.int32)
    at = ids[None, :] - me
    inside = (at >= spans[:, :1]) & (at < spans[:, 1:])
    return jnp.sum(jnp.where(inside, counts[None, :], 0), axis=1)


def local(streams, cotangent, counts, short_filters, long_filter):
    devices = lax.axis_size("ctx")
    me = lax.axis_index("ctx")
    live_count = counts[0, 0]
    share = long_filter.shape[1]
    plan = halo_plan(devices, streams.shape[2])
    digits = jnp.stack([live_count // 16, live_count % 16]).astype(BF16)
    packed = jnp.concatenate(
        [
            long_filter,
            short_filters.reshape(3 * STAP, share),
            jnp.broadcast_to(digits[:, None], (2, share)),
            jnp.zeros((160 - LTAP - 3 * STAP - 2, share), BF16),
        ],
        axis=0,
    )
    tails, heads, filters = exchange(plan, devices, streams, cotangent, counts, packed)
    if share % 128:
        filters = lax.all_gather(packed, "ctx", axis=1, tiled=True)
    digits = filters[LTAP + 3 * STAP : LTAP + 3 * STAP + 2, ::share].astype(jnp.int32)
    info = halo_info(digits[0] * 16 + digits[1], me, plan)
    stream_grads, sums = run_blocks(plan, info, tails, heads, streams, cotangent, filters)
    if share % 128:
        own = lax.psum_scatter(sums, "ctx", scatter_dimension=1, tiled=True)
        squares = lax.psum(jnp.sum(own * own), ("dp", "ctx"))
        own = own / jnp.sqrt(squares / float((LTAP + 3 * STAP) * CH) + 1e-06)
        long_grad, short_rows = own[:LTAP], own[LTAP:]
    else:
        long_grad, short_rows = reduce_sums(sums, devices, lax.axis_size("dp"))
    short_grad = short_rows[: 3 * STAP].reshape(3, STAP, share)
    return (stream_grads, long_grad, short_grad)


def solution(mesh):
    return jax.shard_map(
        local,
        mesh=mesh,
        in_specs=(
            P(None, None, "ctx", "dp"),
            P(None, "ctx", "dp"),
            P(None, "ctx"),
            P(None, None, ("dp", "ctx")),
            P(None, ("dp", "ctx")),
        ),
        out_specs=(
            P(None, None, "ctx", "dp"),
            P(None, ("dp", "ctx")),
            P(None, None, ("dp", "ctx")),
        ),
        check_vma=False,
    )
```
